768 devices in a mesh: row: 64 (over y, x, core), col: 12 (over z).
Axes of the slice: x: 4, y: 8, z: 12, core: 2. Of those that a mesh axis runs over, the one named last changes fastest.
Arguments:
- sketch: float32 [196608, 128], P(('row', 'col')), may hold values from -6 to 6
- degrees: int32 [196608], P(('row', 'col')), may hold values from 1 to 2048, as said below
- tiles: bfloat16 [64, 12, 96, 128, 128], P('row', 'col'), may hold values from -6 to 6
- tile_rows: int32 [64, 12, 96], P('row', 'col'), may hold values from 0 to 23
- tile_peers: int32 [64, 12, 96], P('row', 'col'), may hold values from 0 to 63
- tile_counts: int32 [64, 12], P('row', 'col'), may hold values from 24 to 96, as said below
- requests: int32 [64, 12, 64], P('row', 'col'), may hold values from 0 to 1
Outputs:
- first_basis: float32 [196608, 128], P(('row', 'col'))
- embedding: float32 [196608, 128], P(('row', 'col'))
The draws below stay inside these ranges and needn't reach their ends.
Inputs may be any that keep to these rules, and one draw needn't show every extreme that they name: `degrees`: degrees of every vertex; the largest is reached by some vertex. `tile_counts`: A device holds at most 96 live tiles, and some device holds exactly that many; slots from the count on are ignored. `requests`: every device reads exactly one panel block from every device with its index along col.
All inputs are finite; a program needn't handle non-finite values.
Results may differ from the reference program's by a relative error of at most 0.0042.
Values may be sent and summed in bfloat16 or wider, within the bound.
No kernel may reach another device: no remote copies, remote signals or barrier semaphores. Data moves between devices by JAX's collectives and lax.ppermute only.
A program may use at most 64 MiB of HBM per device.

```python
import jax
import jax.numpy as jnp
from jax import lax

K = 128
TILE = 128
BLK_DEV = 2
TILES_DEV = 96
NV = 196608
N_ROW = 64
N_COL = 12


def draw_degrees(key, part):
    key = jax.random.fold_in(key, 7)
    key_power, key_value, key_spot = jax.random.split(key, 3)
    power = jax.random.randint(key_power, (NV,), 0, 12)
    ceiling = jnp.left_shift(jnp.ones((NV,), jnp.int32), power)
    values = 1 + jax.random.randint(key_value, (NV,), 0, ceiling)
    spot = jax.random.randint(key_spot, (), 0, NV)
    values = jnp.where(jnp.arange(NV) == spot, 2048, values)
    return values.astype(jnp.int32)


def draw_tile_counts(key, part):
    key = jax.random.fold_in(key, 5)
    key_count, key_spot = jax.random.split(key)
    counts = jax.random.randint(key_count, (N_ROW * N_COL,), TILES_DEV // 4, TILES_DEV + 1)
    spot = jax.random.randint(key_spot, (), 0, N_ROW * N_COL)
    counts = jnp.where(jnp.arange(N_ROW * N_COL) == spot, TILES_DEV, counts)
    return counts.reshape(N_ROW, N_COL).astype(jnp.int32)


def with_ends(entries, key, low, top_value):
    extent = entries.shape
    spot = [jax.random.randint(jax.random.fold_in(key, axis), (), 0, extent[axis]) for axis in range(len(extent))]
    entries = entries.at[tuple(spot)].set(low)
    longest = extent.index(max(extent))
    spot[longest] = (spot[longest] + 1) % extent[longest]
    return entries.at[tuple(spot)].set(top_value)


def block_levels(key, shape, shards, low, high):
    gain = 1.0
    for dim, blocks in shards:
        draws = jax.random.uniform(jax.random.fold_in(jax.random.fold_in(key, 6), dim), (blocks,), jnp.float32, low / len(shards), high / len(shards))
        gain = gain * jnp.repeat(jnp.exp(draws), shape[dim] // blocks).reshape((-1,) + (1,) * (len(shape) - 1 - dim))
    return gain


def normal_values(key, dims, scale, bound, shards=(), held_as=jnp.bfloat16):
    array = jax.random.normal(key, dims, jnp.float32) * scale
    if len(shards) > 0:
        array = block_levels(key, dims, shards, -0.22, 0.18) * array
    return jnp.clip(array, min=-bound, max=bound).astype(held_as)


def setup_inputs(seed: int = 0) -> dict:
    key_list = jax.random.split(jax.random.key(seed), 8)
    return {
        "sketch": normal_values(key_list[0], (NV, K), 1.0, 6.0, ((0, 768),), jnp.float32),
        "degrees": draw_degrees(jax.random.fold_in(key_list[7], 71), 0),
        "tiles": normal_values(key_list[2], (N_ROW, N_COL, TILES_DEV, TILE, TILE), 1.0, 6.0, ((0, 64), (1, 12))),
        "tile_rows": with_ends(jax.random.randint(key_list[3], (N_ROW, N_COL, TILES_DEV), 0, N_COL * BLK_DEV), jax.random.fold_in(key_list[3], 1), 0, (N_COL * BLK_DEV) - 1).astype(jnp.int32),
        "tile_peers": with_ends(jax.random.randint(key_list[4], (N_ROW, N_COL, TILES_DEV), 0, N_ROW), jax.random.fold_in(key_list[4], 1), 0, N_ROW - 1).astype(jnp.int32),
        "tile_counts": draw_tile_counts(jax.random.fold_in(key_list[7], 71), 0),
        "requests": with_ends(jax.random.randint(key_list[6], (N_ROW, N_COL, N_ROW), 0, BLK_DEV), jax.random.fold_in(key_list[6], 1), 0, BLK_DEV - 1).astype(jnp.int32),
    }


def apply_operator(panel, tiles, tile_rows, tile_peers, tile_counts, requests):
    blocks = panel.reshape(N_ROW * N_COL * BLK_DEV, TILE, K)

    def one_group(packed):
        group_tiles, rows_here, peer_ids, counts_here, wanted = packed
        columns = jnp.arange(N_COL, dtype=jnp.int32)[:, None]
        chosen = jnp.take_along_axis(wanted, peer_ids, axis=1)
        position = ((peer_ids * N_COL + columns) * BLK_DEV + chosen).astype(jnp.int32)
        sources = blocks[position].astype(jnp.float32)
        products = jnp.einsum('ctij,ctjk->ctik', group_tiles.astype(jnp.float32), sources)
        active = (jnp.arange(TILES_DEV, dtype=jnp.int32)[None, :] < counts_here[:, None]).astype(jnp.float32)
        products = products * active[:, :, None, None]
        return jax.ops.segment_sum(products.reshape(N_COL * TILES_DEV, TILE, K), rows_here.reshape(-1), num_segments=N_COL * BLK_DEV)
    summed = lax.map(one_group, (tiles, tile_rows, tile_peers, tile_counts, requests))
    return summed.reshape(NV, K)

def reference(sketch, degrees, tiles, tile_rows, tile_peers, tile_counts, requests):
    inverse_root = 1.0 / jnp.sqrt(degrees.astype(jnp.float32))
    panel_one = (sketch * inverse_root[:, None]).astype(jnp.bfloat16)
    image_one = apply_operator(panel_one, tiles, tile_rows, tile_peers, tile_counts, requests) * inverse_root[:, None]
    panel_two = (image_one * inverse_root[:, None]).astype(jnp.bfloat16)
    image_two = apply_operator(panel_two, tiles, tile_rows, tile_peers, tile_counts, requests) * inverse_root[:, None]
    gram_one = jnp.dot(image_one.T, image_one, precision=lax.Precision.HIGHEST)
    gram_two = jnp.dot(image_two.T, image_two, precision=lax.Precision.HIGHEST)
    lower_one = jnp.linalg.cholesky(gram_one)
    mixed = jax.scipy.linalg.solve_triangular(lower_one, gram_two, lower=True)
    folded = jax.scipy.linalg.solve_triangular(lower_one, mixed.T, lower=True)
    folded = 0.5 * (folded + folded.T)
    lower_two = jnp.linalg.cholesky(folded)
    factor = jnp.sqrt(jnp.float32(NV))
    first_basis = jax.scipy.linalg.solve_triangular(lower_one, image_one.T, lower=True).T * factor
    partial_solve = jax.scipy.linalg.solve_triangular(lower_one, image_two.T, lower=True)
    embedding = jax.scipy.linalg.solve_triangular(lower_two, partial_solve, lower=True).T * factor
    return (first_basis, embedding)
```

```python
import jax
import jax.numpy as jnp
from jax import lax
from jax.experimental import pallas as pl
from jax.experimental.pallas import tpu as pltpu
from jax.sharding import PartitionSpec as P

TILE = 128
EXTRA = 16
LEVELS = 32766.0
VMEM_LIMIT = 48 * 1024 * 1024


def diagonal_mask():
    return lax.broadcasted_iota(jnp.int32, (TILE, TILE), 0) == lax.broadcasted_iota(
        jnp.int32, (TILE, TILE), 1
    )


def to_lanes(column):
    return jnp.sum(jnp.where(diagonal_mask(), column, 0.0), axis=0, keepdims=True)


def to_sublanes(lanes):
    return jnp.sum(jnp.where(diagonal_mask(), lanes, 0.0), axis=1, keepdims=True)


def gram_of(image):
    return lax.dot_general(
        image,
        image,
        (((0,), (0,)), ((), ())),
        precision=lax.Precision.HIGHEST,
        preferred_element_type=jnp.float32,
    )


def write_requested(requested, panel, outgoing_ref):
    for peer in range(outgoing_ref.shape[0]):
        outgoing_ref[peer] = jnp.where(requested[peer] == 0, panel[:TILE], panel[TILE:])


def first_panel_kernel(requested, sketch_ref, root_ref, outgoing_ref):
    panel = (sketch_ref[...] * root_ref[...]).astype(jnp.bfloat16)
    write_requested(requested, panel, outgoing_ref)


def product_kernel(rows, sources, count, tiles_ref, arrived_ref, coded_ref, total):
    unroll = 8
    total[...] = jnp.zeros_like(total)

    def steps(group, carry):
        for k in range(unroll):
            slot = group * unroll + k
            row = rows[slot]
            total[row] += jnp.dot(
                tiles_ref[slot], arrived_ref[sources[slot]], preferred_element_type=jnp.float32
            )
        return carry

    lax.fori_loop(0, (count[0] + unroll - 1) // unroll, steps, 0)
    holders, coded_rows, _ = coded_ref.shape
    blocks = (coded_rows - EXTRA) // TILE
    line = lax.broadcasted_iota(jnp.int32, (EXTRA, TILE), 0)

    def code(holder, carry):
        exponents = jnp.zeros((EXTRA, TILE), jnp.float32)
        for b in range(blocks):
            value = total[holder * blocks + b]
            top = jnp.max(jnp.abs(value), axis=1, keepdims=True)
            exponent = jnp.ceil(jnp.log2(jnp.clip(top, 2.0**-100, 2.0**120)))
            scaled = value * (jnp.exp2(-exponent) * LEVELS)
            scaled = jnp.clip(jnp.floor(scaled + 0.5), -32767.0, 32767.0)
            coded_ref[holder, b * TILE : (b + 1) * TILE, :] = scaled.astype(jnp.int32).astype(jnp.int16)
            exponents = jnp.where(line == b, to_lanes(exponent), exponents)
        coded_ref[holder, blocks * TILE :, :] = exponents.astype(jnp.int32).astype(jnp.int16)
        return carry

    lax.fori_loop(0, holders, code, 0)


def decode(coded_ref, root_ref):
    holders, coded_rows, _ = coded_ref.shape
    blocks = (coded_rows - EXTRA) // TILE
    sums = [jnp.zeros((TILE, TILE), jnp.float32)] * blocks
    for holder in range(holders):
        exponents = coded_ref[holder, blocks * TILE :, :].astype(jnp.int32).astype(jnp.float32)
        for b in range(blocks):
            scale = jnp.exp2(to_sublanes(exponents[b : b + 1])) * (1.0 / LEVELS)
            value = coded_ref[holder, b * TILE : (b + 1) * TILE, :].astype(jnp.int32).astype(jnp.float32)
            sums[b] = sums[b] + value * scale
    return jnp.concatenate(sums, axis=0) * root_ref[...]


def middle_kernel(requested, coded_ref, root_ref, image_ref, gram_ref, outgoing_ref):
    image = decode(coded_ref, root_ref)
    image_ref[...] = image
    panel = (image * root_ref[...]).astype(jnp.bfloat16)
    write_requested(requested, panel, outgoing_ref)
    gram_ref[...] = gram_of(image)


def last_kernel(coded_ref, root_ref, image_ref, gram_ref):
    image = decode(coded_ref, root_ref)
    image_ref[...] = image
    gram_ref[...] = gram_of(image)


def call(kernel, out_shape, n_scalars, n_inputs, scratch=()):
    single = isinstance(out_shape, jax.ShapeDtypeStruct)
    return pl.pallas_call(
        kernel,
        out_shape=out_shape,
        in_specs=[pl.BlockSpec(memory_space=pltpu.SMEM)] * n_scalars
        + [pl.BlockSpec(memory_space=pltpu.VMEM)] * n_inputs,
        out_specs=pl.BlockSpec(memory_space=pltpu.VMEM)
        if single
        else [pl.BlockSpec(memory_space=pltpu.VMEM)] * len(out_shape),
        scratch_shapes=list(scratch),
        compiler_params=pltpu.CompilerParams(vmem_limit_bytes=VMEM_LIMIT),
    )


def sum_over_devices(value, row_devices, col_devices):
    rows, width = value.shape
    share = rows // row_devices
    parts = lax.all_to_all(
        value.reshape(row_devices, share, width), "row", split_axis=0, concat_axis=0, tiled=True
    )
    part = jnp.sum(parts, axis=0)
    parts = lax.all_to_all(
        jnp.broadcast_to(part[None], (col_devices, share, width)), "col", split_axis=0, concat_axis=0, tiled=True
    )
    part = jnp.sum(parts, axis=0)
    parts = lax.all_to_all(
        jnp.broadcast_to(part[None], (row_devices, share, width)), "row", split_axis=0, concat_axis=0, tiled=True
    )
    return parts.reshape(rows, width)


def on_device(sketch, degrees, tiles, tile_rows, tile_peers, tile_counts, requests):
    rows_dev, width = sketch.shape
    slots = tiles.shape[2]
    row_devices = lax.axis_size("row")
    col_devices = lax.axis_size("col")
    blocks_dev = rows_dev // TILE
    group_blocks = col_devices * blocks_dev
    f32, bf16, i16 = jnp.float32, jnp.bfloat16, jnp.int16
    shape = jax.ShapeDtypeStruct

    inverse_root = 1.0 / jnp.sqrt(degrees.astype(f32))
    root = jnp.broadcast_to(inverse_root[:, None], (rows_dev, width))
    own_tiles = tiles[0, 0]
    count = tile_counts[0]
    live = jnp.arange(slots, dtype=jnp.int32) < count
    row_ids = jnp.where(live, tile_rows[0, 0], group_blocks)
    source_ids = tile_peers[0, 0]
    requested = lax.all_to_all(
        requests[0, 0].reshape(row_devices, 1), "row", split_axis=0, concat_axis=0, tiled=True
    ).reshape(row_devices)

    outgoing_shape = shape((row_devices, TILE, width), bf16)
    coded_shape = shape((col_devices, rows_dev + EXTRA, width), i16)
    image_shape = shape((rows_dev, width), f32)
    gram_shape = shape((width, width), f32)
    total = pltpu.VMEM((group_blocks + 1, TILE, width), f32)

    def product(outgoing):
        arrived = lax.all_to_all(outgoing, "row", split_axis=0, concat_axis=0, tiled=True)
        coded = call(product_kernel, coded_shape, 3, 2, [total])(
            row_ids, source_ids, count, own_tiles, arrived
        )
        return lax.all_to_all(coded, "col", split_axis=0, concat_axis=0, tiled=True)

    outgoing = call(first_panel_kernel, outgoing_shape, 1, 2)(requested, sketch, root)
    terms = product(outgoing)
    image_one, gram_one, outgoing = call(
        middle_kernel, (image_shape, gram_shape, outgoing_shape), 1, 2
    )(requested, terms, root)
    terms = product(outgoing)
    image_two, gram_two = call(last_kernel, (image_shape, gram_shape), 0, 2)(terms, root)

    grams = sum_over_devices(jnp.concatenate([gram_one, gram_two], axis=1), row_devices, col_devices)
    gram_one, gram_two = grams[:, :width], grams[:, width:]
    lower_one = jnp.linalg.cholesky(gram_one)
    mixed = jax.scipy.linalg.solve_triangular(lower_one, gram_two, lower=True)
    folded = jax.scipy.linalg.solve_triangular(lower_one, mixed.T, lower=True)
    folded = 0.5 * (folded + folded.T)
    lower_two = jnp.linalg.cholesky(folded)
    factor = jnp.sqrt(f32(rows_dev * row_devices * col_devices))
    first_basis = jax.scipy.linalg.solve_triangular(lower_one, image_one.T, lower=True).T * factor
    partial_solve = jax.scipy.linalg.solve_triangular(lower_one, image_two.T, lower=True)
    embedding = jax.scipy.linalg.solve_triangular(lower_two, partial_solve, lower=True).T * factor
    return (first_basis, embedding)


def solution(mesh):
    return jax.shard_map(
        on_device,
        mesh=mesh,
        in_specs=(
            P(("row", "col"), None),
            P(("row", "col")),
            P("row", "col", None, None, None),
            P("row", "col", None),
            P("row", "col", None),
            P("row", "col"),
            P("row", "col", None),
        ),
        out_specs=(P(("row", "col"), None), P(("row", "col"), None)),
        check_vma=False,
    )
```

```python
import functools

import jax
import jax.numpy as jnp
from jax import lax
from jax.experimental import pallas as pl
from jax.experimental.pallas import tpu as pltpu
from jax.sharding import PartitionSpec as P

TILE = 128
EXTRA = 16
LEVELS = 32766.0
VMEM_LIMIT = 48 * 1024 * 1024
SUBLANES = 8
CORES = 2
CHIPS_X = 4
PLANE = CHIPS_X * CORES


def diagonal_mask():
    return lax.broadcasted_iota(jnp.int32, (TILE, TILE), 0) == lax.broadcasted_iota(
        jnp.int32, (TILE, TILE), 1
    )


def to_lanes(column):
    return jnp.sum(jnp.where(diagonal_mask(), column, 0.0), axis=0, keepdims=True)


def to_sublanes(lanes):
    return jnp.sum(jnp.where(diagonal_mask(), lanes, 0.0), axis=1, keepdims=True)


def write_copies(panel, copies_ref):
    for y in range(copies_ref.shape[0]):
        copies_ref[y] = panel


def first_panel_kernel(sketch_ref, root_ref, copies_ref):
    write_copies((sketch_ref[...] * root_ref[...]).astype(jnp.bfloat16), copies_ref)


def select_kernel(wanted, row, panels_ref, outgoing_ref):
    planes = panels_ref.shape[0]
    place = row[0] % PLANE
    x = place // CORES
    rows = planes * PLANE
    for g in range(PLANE):
        shift = (x - g // CORES + CHIPS_X) % CHIPS_X
        base = (shift * CORES + g % CORES) * rows + place
        for y in range(planes):
            outgoing_ref[g, y] = panels_ref[y, wanted[base + y * PLANE]]


def product_kernel(rows, peers, count, tiles_ref, arrived_ref, coded_ref, total):
    unroll = 8
    holders, coded_rows, _ = coded_ref.shape
    blocks = (coded_rows - EXTRA) // TILE
    spare = holders * blocks
    planes = arrived_ref.shape[0] // PLANE
    total[...] = jnp.zeros_like(total)

    def steps(group, carry):
        for k in range(unroll):
            slot = group * unroll + k
            row = jnp.where(slot < count[0], rows[slot], spare)
            peer = peers[slot]
            source = peer % PLANE * planes + peer // PLANE
            total[row] += jnp.dot(
                tiles_ref[slot], arrived_ref[source], preferred_element_type=jnp.float32
            )
        return carry

    lax.fori_loop(0, (count[0] + unroll - 1) // unroll, steps, 0)
    line = lax.broadcasted_iota(jnp.int32, (EXTRA, TILE), 0)
    for holder in range(holders):
        exponents = jnp.zeros((EXTRA, TILE), jnp.float32)
        for b in range(blocks):
            value = total[holder * blocks + b]
            top = jnp.max(jnp.abs(value), axis=1, keepdims=True)
            exponent = jnp.ceil(jnp.log2(jnp.clip(top, 2.0**-100, 2.0**120)))
            scaled = value * (jnp.exp2(-exponent) * LEVELS)
            scaled = jnp.clip(jnp.round(scaled), -32767.0, 32767.0)
            coded_ref[holder, b * TILE : (b + 1) * TILE, :] = scaled.astype(jnp.int32).astype(jnp.int16)
            exponents = jnp.where(line == b, to_lanes(exponent), exponents)
        coded_ref[holder, blocks * TILE :, :] = exponents.astype(jnp.int32).astype(jnp.int16)


def decode(coded_ref, root_ref):
    holders, coded_rows, _ = coded_ref.shape
    blocks = (coded_rows - EXTRA) // TILE
    sums = [jnp.zeros((TILE, TILE), jnp.float32)] * blocks
    for holder in range(holders):
        exponents = coded_ref[holder, blocks * TILE :, :].astype(jnp.int32).astype(jnp.float32)
        for b in range(blocks):
            scale = jnp.exp2(to_sublanes(exponents[b : b + 1])) * (1.0 / LEVELS)
            value = coded_ref[holder, b * TILE : (b + 1) * TILE, :].astype(jnp.int32).astype(jnp.float32)
            sums[b] = sums[b] + value * scale
    return jnp.concatenate(sums, axis=0) * root_ref[...]


def middle_kernel(coded_ref, root_ref, image_ref, gram_ref, copies_ref):
    image = decode(coded_ref, root_ref)
    image_ref[...] = image
    write_copies((image * root_ref[...]).astype(jnp.bfloat16), copies_ref)
    gram_ref[...] = dot(image, image, 0, 0)


def last_kernel(coded_ref, root_ref, image_ref, gram_ref):
    image = decode(coded_ref, root_ref)
    image_ref[...] = image
    gram_ref[...] = dot(image, image, 0, 0)


def dot(a, b, a_dim, b_dim):
    return lax.dot_general(
        a,
        b,
        (((a_dim,), (b_dim,)), ((), ())),
        precision=lax.Precision.HIGHEST,
        preferred_element_type=jnp.float32,
    )


def inverse_cholesky(gram):
    size = gram.shape[0]
    band = (SUBLANES, size)
    lane = lax.broadcasted_iota(jnp.int32, band, 1)
    line = lax.broadcasted_iota(jnp.int32, band, 0)
    steps = range(size // SUBLANES)
    inner = range(SUBLANES)
    left = [gram[SUBLANES * k : SUBLANES * (k + 1)] for k in steps]
    right = [(lane == line + SUBLANES * k).astype(jnp.float32) for k in steps]

    def spread(rows, column):
        return jnp.broadcast_to(rows[:, column : column + 1], band)

    for k in steps:
        start = SUBLANES * k
        row_left = [jnp.broadcast_to(left[k][j : j + 1], band) for j in inner]
        row_right = [jnp.broadcast_to(right[k][j : j + 1], band) for j in inner]
        entry = [[spread(row_left[j], start + t) if t >= j else None for t in inner] for j in inner]
        inverse = [None] * SUBLANES
        factor = [[None] * SUBLANES for _ in inner]
        for j in inner:
            inverse[j] = 1.0 / entry[j][j]
            for t in range(j + 1, SUBLANES):
                factor[t][j] = entry[j][t] * inverse[j]
                for u in range(t, SUBLANES):
                    entry[t][u] = entry[t][u] - factor[t][j] * entry[j][u]
                row_left[t] = row_left[t] - factor[t][j] * row_left[j]
                row_right[t] = row_right[t] - factor[t][j] * row_right[j]
        step_left = [row_left[j] * inverse[j] for j in inner]
        step_right = [row_right[j] * inverse[j] for j in inner]
        for q in steps[k + 1 :]:
            column = [spread(left[q], start + j) for j in inner]
            for j in inner:
                for t in range(j + 1, SUBLANES):
                    column[t] = column[t] - column[j] * factor[t][j]
            left[q] = left[q] - sum(column[j] * step_left[j] for j in inner)
            right[q] = right[q] - sum(column[j] * step_right[j] for j in inner)
        for j in inner:
            right[k] = jnp.where(line == j, row_right[j] * lax.rsqrt(entry[j][j]), right[k])
    return jnp.concatenate(right, axis=0)


def bases_kernel(scale, grams_ref, image_one_ref, image_two_ref, first_ref, second_ref):
    width = grams_ref.shape[0]
    inverse_one = inverse_cholesky(grams_ref[:, :width])
    partial_solve = dot(image_two_ref[...], inverse_one, 1, 1)
    first_ref[...] = dot(image_one_ref[...], inverse_one, 1, 1) * scale
    folded = dot(dot(inverse_one, grams_ref[:, width:], 1, 0), inverse_one, 1, 1)
    folded = 0.5 * (folded + folded.T)
    inverse_two = inverse_cholesky(folded)
    second_ref[...] = dot(partial_solve, inverse_two, 1, 1) * scale


def call(kernel, out_shape, n_scalars, n_inputs, scratch=()):
    single = isinstance(out_shape, jax.ShapeDtypeStruct)
    return pl.pallas_call(
        kernel,
        out_shape=out_shape,
        in_specs=[pl.BlockSpec(memory_space=pltpu.SMEM)] * n_scalars
        + [pl.BlockSpec(memory_space=pltpu.VMEM)] * n_inputs,
        out_specs=pl.BlockSpec(memory_space=pltpu.VMEM)
        if single
        else [pl.BlockSpec(memory_space=pltpu.VMEM)] * len(out_shape),
        scratch_shapes=list(scratch),
        compiler_params=pltpu.CompilerParams(vmem_limit_bytes=VMEM_LIMIT),
    )


def sum_over_devices(value, row_devices, col_devices):
    rows, width = value.shape
    share = rows // row_devices
    parts = lax.all_to_all(
        value.reshape(row_devices, share, width), "row", split_axis=0, concat_axis=0, tiled=True
    )
    part = jnp.sum(parts, axis=0)
    parts = lax.all_to_all(
        jnp.broadcast_to(part[None], (col_devices, share, width)), "col", split_axis=0, concat_axis=0, tiled=True
    )
    part = jnp.sum(parts, axis=0)
    parts = lax.all_to_all(
        jnp.broadcast_to(part[None], (row_devices, share, width)), "row", split_axis=0, concat_axis=0, tiled=True
    )
    return parts.reshape(rows, width)


def on_device(sketch, degrees, tiles, tile_rows, tile_peers, tile_counts, requests):
    rows_dev, width = sketch.shape
    row_devices = lax.axis_size("row")
    col_devices = lax.axis_size("col")
    blocks_dev = rows_dev // TILE
    group_blocks = col_devices * blocks_dev
    f32, bf16, i16 = jnp.float32, jnp.bfloat16, jnp.int16
    shape = jax.ShapeDtypeStruct

    inverse_root = 1.0 / jnp.sqrt(degrees.astype(f32))
    own_tiles = tiles[0, 0]
    count = tile_counts[0]
    planes = row_devices // PLANE
    row = lax.axis_index("row").reshape(1)

    mine = requests[0, 0]
    other = lax.ppermute(mine, "row", [(r, r ^ 1) for r in range(row_devices)])
    even = row[0] % CORES == 0
    pair = jnp.concatenate([jnp.where(even, mine, other), jnp.where(even, other, mine)])
    root = jnp.broadcast_to(inverse_root[:, None], (rows_dev, width))
    copies_shape = shape((planes, rows_dev, width), bf16)
    copies = call(first_panel_kernel, copies_shape, 0, 2)(sketch, root)
    pair, copies = lax.optimization_barrier((pair, copies))
    tables = [pair]
    for shift in range(1, CHIPS_X):
        tables.append(
            lax.ppermute(
                pair,
                "row",
                [
                    (r, r // PLANE * PLANE + (r + shift * CORES) % PLANE)
                    for r in range(row_devices)
                ],
            )
        )
    wanted = jnp.concatenate(tables)
    lines = [[y * PLANE + g for y in range(planes)] for g in range(PLANE)]
    plane = [[y * PLANE + g for g in range(PLANE)] for y in range(planes)]

    outgoing_shape = shape((PLANE, planes, TILE, width), bf16)
    coded_shape = shape((col_devices, rows_dev + EXTRA, width), i16)
    image_shape = shape((rows_dev, width), f32)
    gram_shape = shape((width, width), f32)
    total = pltpu.VMEM((group_blocks + 1, TILE, width), f32)

    def product(copies):
        panels = lax.all_to_all(
            copies, "row", split_axis=0, concat_axis=0, tiled=True, axis_index_groups=lines
        ).reshape(planes, blocks_dev, TILE, width)
        outgoing = call(select_kernel, outgoing_shape, 2, 1)(wanted, row, panels)
        arrived = lax.all_to_all(
            outgoing, "row", split_axis=0, concat_axis=0, tiled=True, axis_index_groups=plane
        ).reshape(row_devices, TILE, width)
        coded = call(product_kernel, coded_shape, 3, 2, [total])(
            tile_rows[0, 0], tile_peers[0, 0], count, own_tiles, arrived
        )
        return lax.all_to_all(coded, "col", split_axis=0, concat_axis=0, tiled=True)

    terms = product(copies)
    image_one, gram_one, copies = call(
        middle_kernel, (image_shape, gram_shape, copies_shape), 0, 2
    )(terms, root)
    terms = product(copies)
    image_two, gram_two = call(last_kernel, (image_shape, gram_shape), 0, 2)(terms, root)

    grams = sum_over_devices(jnp.concatenate([gram_one, gram_two], axis=1), row_devices, col_devices)
    scale = (rows_dev * row_devices * col_devices) ** 0.5
    return call(functools.partial(bases_kernel, scale), (image_shape, image_shape), 0, 3)(
        grams, image_one, image_two
    )


def solution(mesh):
    return jax.shard_map(
        on_device,
        mesh=mesh,
        in_specs=(
            P(("row", "col"), None),
            P(("row", "col")),
            P("row", "col", None, None, None),
            P("row", "col", None),
            P("row", "col", None),
            P("row", "col"),
            P("row", "col", None),
        ),
        out_specs=(P(("row", "col"), None), P(("row", "col"), None)),
        check_vma=False,
    )
```

```python
import functools

import jax
import jax.numpy as jnp
from jax import lax
from jax.experimental import pallas as pl
from jax.experimental.pallas import tpu as pltpu
from jax.sharding import PartitionSpec as P

TILE = 128
EXTRA = 16
LEVELS = 32766.0
VMEM_LIMIT = 48 * 1024 * 1024
SUBLANES = 8
CORES = 2
CHIPS_X = 4
PLANE = CHIPS_X * CORES


def diagonal_mask():
    return lax.broadcasted_iota(jnp.int32, (TILE, TILE), 0) == lax.broadcasted_iota(
        jnp.int32, (TILE, TILE), 1
    )


def to_lanes(column):
    return jnp.sum(jnp.where(diagonal_mask(), column, 0.0), axis=0, keepdims=True)


def to_sublanes(lanes):
    return jnp.sum(jnp.where(diagonal_mask(), lanes, 0.0), axis=1, keepdims=True)


def write_copies(panel, copies_ref):
    for y in range(copies_ref.shape[0]):
        copies_ref[y] = panel


def first_panel_kernel(degrees_ref, sketch_ref, copies_ref, root_ref, sketch, arrival):
    copy = pltpu.make_async_copy(sketch_ref, sketch, arrival)
    copy.start()
    roots = lax.rsqrt(degrees_ref[...].astype(jnp.float32))
    for b in range(degrees_ref.shape[0]):
        column = to_sublanes(roots[b : b + 1])
        root_ref[b * TILE : (b + 1) * TILE] = jnp.broadcast_to(column, (TILE, root_ref.shape[1]))
    copy.wait()
    write_copies((sketch[...] * root_ref[...]).astype(jnp.bfloat16), copies_ref)


def select_kernel(wanted, row, panels_ref, outgoing_ref):
    planes = panels_ref.shape[0]
    place = row[0] % PLANE
    x = place // CORES
    rows = planes * PLANE
    for g in range(PLANE):
        shift = (x - g // CORES + CHIPS_X) % CHIPS_X
        side = (place + g) % CORES
        base = (shift * CORES + side) * rows + place
        for y in range(planes):
            outgoing_ref[g, y] = panels_ref[y, wanted[base + y * PLANE]]


def product_kernel(plan, tiles_ref, arrived_ref, coded_ref, total):
    unroll = 32
    slots = tiles_ref.shape[0]
    count = plan[2 * slots]
    holders, coded_rows, _ = coded_ref.shape
    blocks = (coded_rows - EXTRA) // TILE
    spare = holders * blocks
    planes = arrived_ref.shape[0] // PLANE
    total[...] = jnp.zeros_like(total)

    def steps(group, carry):
        for k in range(unroll):
            slot = group * unroll + k
            row = jnp.where(slot < count, plan[slot], spare)
            peer = plan[slots + slot]
            source = peer % PLANE * planes + peer // PLANE
            total[row] += jnp.dot(
                tiles_ref[slot], arrived_ref[source], preferred_element_type=jnp.float32
            )
        return carry

    lax.fori_loop(0, (count + unroll - 1) // unroll, steps, 0)
    line = lax.broadcasted_iota(jnp.int32, (EXTRA, TILE), 0)
    for holder in range(holders):
        exponents = jnp.zeros((EXTRA, TILE), jnp.float32)
        for b in range(blocks):
            value = total[holder * blocks + b]
            top = jnp.max(jnp.abs(value), axis=1, keepdims=True)
            exponent = jnp.ceil(jnp.log2(jnp.clip(top, 2.0**-100, 2.0**120)))
            scaled = value * (jnp.exp2(-exponent) * LEVELS)
            scaled = jnp.clip(jnp.round(scaled), -32767.0, 32767.0)
            coded_ref[holder, b * TILE : (b + 1) * TILE, :] = scaled.astype(jnp.int32).astype(jnp.int16)
            exponents = jnp.where(line == b, to_lanes(exponent), exponents)
        coded_ref[holder, blocks * TILE :, :] = exponents.astype(jnp.int32).astype(jnp.int16)


def decode(coded_ref, root_ref):
    holders, coded_rows, _ = coded_ref.shape
    blocks = (coded_rows - EXTRA) // TILE
    sums = [jnp.zeros((TILE, TILE), jnp.float32)] * blocks
    for holder in range(holders):
        exponents = coded_ref[holder, blocks * TILE :, :].astype(jnp.int32).astype(jnp.float32)
        for b in range(blocks):
            scale = jnp.exp2(to_sublanes(exponents[b : b + 1])) * (1.0 / LEVELS)
            value = coded_ref[holder, b * TILE : (b + 1) * TILE, :].astype(jnp.int32).astype(jnp.float32)
            sums[b] = sums[b] + value * scale
    return jnp.concatenate(sums, axis=0) * root_ref[...]


def middle_kernel(coded_ref, root_ref, image_ref, gram_ref, copies_ref):
    image = decode(coded_ref, root_ref)
    image_ref[...] = image
    write_copies((image * root_ref[...]).astype(jnp.bfloat16), copies_ref)
    gram_ref[...] = dot(image, image, 0, 0)


def last_kernel(coded_ref, root_ref, image_ref, gram_ref):
    image = decode(coded_ref, root_ref)
    image_ref[...] = image
    gram_ref[...] = dot(image, image, 0, 0)


def dot(a, b, a_dim, b_dim):
    return lax.dot_general(
        a,
        b,
        (((a_dim,), (b_dim,)), ((), ())),
        precision=lax.Precision.HIGHEST,
        preferred_element_type=jnp.float32,
    )


def inverse_cholesky(gram):
    size = gram.shape[0]
    band = (SUBLANES, size)
    lane = lax.broadcasted_iota(jnp.int32, band, 1)
    line = lax.broadcasted_iota(jnp.int32, band, 0)
    steps = range(size // SUBLANES)
    inner = range(SUBLANES)
    left = [gram[SUBLANES * k : SUBLANES * (k + 1)] for k in steps]
    right = [(lane == line + SUBLANES * k).astype(jnp.float32) for k in steps]

    def spread(rows, column):
        return jnp.broadcast_to(rows[:, column : column + 1], band)

    for k in steps:
        start = SUBLANES * k
        row_left = [jnp.broadcast_to(left[k][j : j + 1], band) for j in inner]
        row_right = [jnp.broadcast_to(right[k][j : j + 1], band) for j in inner]
        entry = [[spread(row_left[j], start + t) if t >= j else None for t in inner] for j in inner]
        inverse = [None] * SUBLANES
        factor = [[None] * SUBLANES for _ in inner]
        for j in inner:
            inverse[j] = 1.0 / entry[j][j]
            for t in range(j + 1, SUBLANES):
                factor[t][j] = entry[j][t] * inverse[j]
                for u in range(t, SUBLANES):
                    entry[t][u] = entry[t][u] - factor[t][j] * entry[j][u]
                row_left[t] = row_left[t] - factor[t][j] * row_left[j]
                row_right[t] = row_right[t] - factor[t][j] * row_right[j]
        step_left = [row_left[j] * inverse[j] for j in inner]
        step_right = [row_right[j] * inverse[j] for j in inner]
        for q in steps[k + 1 :]:
            column = [spread(left[q], start + j) for j in inner]
            for j in inner:
                for t in range(j + 1, SUBLANES):
                    column[t] = column[t] - column[j] * factor[t][j]
            left[q] = left[q] - sum(column[j] * step_left[j] for j in inner)
            right[q] = right[q] - sum(column[j] * step_right[j] for j in inner)
        for j in inner:
            right[k] = jnp.where(line == j, row_right[j] * lax.rsqrt(entry[j][j]), right[k])
    return jnp.concatenate(right, axis=0)


def bases_kernel(scale, grams_ref, image_one_ref, image_two_ref, first_ref, second_ref):
    width = grams_ref.shape[0]
    inverse_one = inverse_cholesky(grams_ref[:, :width])
    partial_solve = dot(image_two_ref[...], inverse_one, 1, 1)
    first_ref[...] = dot(image_one_ref[...], inverse_one, 1, 1) * scale
    folded = dot(dot(inverse_one, grams_ref[:, width:], 1, 0), inverse_one, 1, 1)
    folded = 0.5 * (folded + folded.T)
    inverse_two = inverse_cholesky(folded)
    second_ref[...] = dot(partial_solve, inverse_two, 1, 1) * scale


def call(kernel, out_shape, n_scalars, n_inputs, scratch=()):
    single = isinstance(out_shape, jax.ShapeDtypeStruct)
    return pl.pallas_call(
        kernel,
        out_shape=out_shape,
        in_specs=[pl.BlockSpec(memory_space=pltpu.SMEM)] * n_scalars
        + [pl.BlockSpec(memory_space=pltpu.VMEM)] * n_inputs,
        out_specs=pl.BlockSpec(memory_space=pltpu.VMEM)
        if single
        else [pl.BlockSpec(memory_space=pltpu.VMEM)] * len(out_shape),
        scratch_shapes=list(scratch),
        compiler_params=pltpu.CompilerParams(vmem_limit_bytes=VMEM_LIMIT),
    )


def sum_over_devices(value, row_devices, col_devices):
    rows, width = value.shape
    share = rows // row_devices
    parts = lax.all_to_all(
        value.reshape(row_devices, share, width), "row", split_axis=0, concat_axis=0, tiled=True
    )
    part = jnp.sum(parts, axis=0)
    parts = lax.all_to_all(
        jnp.broadcast_to(part[None], (col_devices, share, width)), "col", split_axis=0, concat_axis=0, tiled=True
    )
    part = jnp.sum(parts, axis=0)
    parts = lax.all_to_all(
        jnp.broadcast_to(part[None], (row_devices, share, width)), "row", split_axis=0, concat_axis=0, tiled=True
    )
    return parts.reshape(rows, width)


def on_device(sketch, degrees, tiles, tile_rows, tile_peers, tile_counts, requests):
    rows_dev, width = sketch.shape
    row_devices = lax.axis_size("row")
    col_devices = lax.axis_size("col")
    blocks_dev = rows_dev // TILE
    group_blocks = col_devices * blocks_dev
    f32, bf16, i16 = jnp.float32, jnp.bfloat16, jnp.int16
    shape = jax.ShapeDtypeStruct
    own_tiles = tiles[0, 0]
    planes = row_devices // PLANE
    row = lax.axis_index("row").reshape(1)

    copies_shape = shape((planes, rows_dev, width), bf16)
    image_shape = shape((rows_dev, width), f32)
    copies, root = pl.pallas_call(
        first_panel_kernel,
        out_shape=(copies_shape, image_shape),
        in_specs=[pl.BlockSpec(memory_space=pltpu.VMEM), pl.BlockSpec(memory_space=pl.ANY)],
        out_specs=[pl.BlockSpec(memory_space=pltpu.VMEM)] * 2,
        scratch_shapes=[pltpu.VMEM((rows_dev, width), f32), pltpu.SemaphoreType.DMA],
        compiler_params=pltpu.CompilerParams(vmem_limit_bytes=VMEM_LIMIT),
    )(degrees.reshape(blocks_dev, TILE), sketch)

    mine = requests[0, 0]
    other = lax.ppermute(mine, "row", [(r, r ^ 1) for r in range(row_devices)])
    pair, copies = lax.optimization_barrier((jnp.concatenate([mine, other]), copies))
    tables = [pair]
    for shift in range(1, CHIPS_X):
        tables.append(
            lax.ppermute(
                pair,
                "row",
                [
                    (r, r // PLANE * PLANE + (r + shift * CORES) % PLANE)
                    for r in range(row_devices)
                ],
            )
        )
    wanted, plan = lax.optimization_barrier(
        (
            jnp.concatenate(tables),
            jnp.concatenate([tile_rows[0, 0], tile_peers[0, 0], tile_counts[0]]),
        )
    )
    lines = [[y * PLANE + g for y in range(planes)] for g in range(PLANE)]
    plane = [[y * PLANE + g for g in range(PLANE)] for y in range(planes)]

    outgoing_shape = shape((PLANE, planes, TILE, width), bf16)
    coded_shape = shape((col_devices, rows_dev + EXTRA, width), i16)
    gram_shape = shape((width, width), f32)
    total = pltpu.VMEM((group_blocks + 1, TILE, width), f32)

    def product(copies):
        panels = lax.all_to_all(
            copies, "row", split_axis=0, concat_axis=0, tiled=True, axis_index_groups=lines
        ).reshape(planes, blocks_dev, TILE, width)
        outgoing = call(select_kernel, outgoing_shape, 2, 1)(wanted, row, panels)
        arrived = lax.all_to_all(
            outgoing, "row", split_axis=0, concat_axis=0, tiled=True, axis_index_groups=plane
        ).reshape(row_devices, TILE, width)
        coded = call(product_kernel, coded_shape, 1, 2, [total])(plan, own_tiles, arrived)
        return lax.all_to_all(coded, "col", split_axis=0, concat_axis=0, tiled=True)

    terms = product(copies)
    image_one, gram_one, copies = call(
        middle_kernel, (image_shape, gram_shape, copies_shape), 0, 2
    )(terms, root)
    terms = product(copies)
    image_two, gram_two = call(last_kernel, (image_shape, gram_shape), 0, 2)(terms, root)

    grams = sum_over_devices(jnp.concatenate([gram_one, gram_two], axis=1), row_devices, col_devices)
    scale = (rows_dev * row_devices * col_devices) ** 0.5
    return call(functools.partial(bases_kernel, scale), (image_shape, image_shape), 0, 3)(
        grams, image_one, image_two
    )


def solution(mesh):
    return jax.shard_map(
        on_device,
        mesh=mesh,
        in_specs=(
            P(("row", "col"), None),
            P(("row", "col")),
            P("row", "col", None, None, None),
            P("row", "col", None),
            P("row", "col", None),
            P("row", "col"),
            P("row", "col", None),
        ),
        out_specs=(P(("row", "col"), None), P(("row", "col"), None)),
        check_vma=False,
    )
```

```python
import functools

import jax
import jax.numpy as jnp
from jax import lax
from jax.experimental import pallas as pl
from jax.experimental.pallas import tpu as pltpu
from jax.sharding import PartitionSpec as P

TILE = 128
EXTRA = 16
LEVELS = 32766.0
VMEM_LIMIT = 48 * 1024 * 1024
SUBLANES = 8
CORES = 2
CHIPS_X = 4
PLANE = CHIPS_X * CORES


def diagonal_mask():
    return lax.broadcasted_iota(jnp.int32, (TILE, TILE), 0) == lax.broadcasted_iota(
        jnp.int32, (TILE, TILE), 1
    )


def to_lanes(column):
    return jnp.sum(jnp.where(diagonal_mask(), column, 0.0), axis=0, keepdims=True)


def to_sublanes(lanes):
    return jnp.sum(jnp.where(diagonal_mask(), lanes, 0.0), axis=1, keepdims=True)


def write_copies(panel, copies_ref):
    for y in range(copies_ref.shape[0]):
        copies_ref[y] = panel


def first_panel_kernel(degrees_ref, sketch_ref, copies_ref, root_ref, sketch, arrival):
    copy = pltpu.make_async_copy(sketch_ref, sketch, arrival)
    copy.start()
    roots = lax.rsqrt(degrees_ref[...].astype(jnp.float32))
    for b in range(degrees_ref.shape[0]):
        column = to_sublanes(roots[b : b + 1])
        root_ref[b * TILE : (b + 1) * TILE] = jnp.broadcast_to(column, (TILE, root_ref.shape[1]))
    copy.wait()
    write_copies((sketch[...] * root_ref[...]).astype(jnp.bfloat16), copies_ref)


def select_kernel(wanted, row, panels_ref, outgoing_ref):
    planes = panels_ref.shape[0]
    place = row[0] % PLANE
    x = place // CORES
    rows = planes * PLANE
    for g in range(PLANE):
        shift = (x - g // CORES + CHIPS_X) % CHIPS_X
        side = (place + g) % CORES
        base = (shift * CORES + side) * rows + place
        for y in range(planes):
            outgoing_ref[g, y] = panels_ref[y, wanted[base + y * PLANE]]


def product_kernel(plan, tiles_ref, arrived_ref, coded_ref, total):
    unroll = 32
    slots = tiles_ref.shape[0]
    count = plan[2 * slots]
    holders, coded_rows, _ = coded_ref.shape
    blocks = (coded_rows - EXTRA) // TILE
    spare = holders * blocks
    planes = arrived_ref.shape[0] // PLANE
    total[...] = jnp.zeros_like(total)

    def steps(group, carry):
        for k in range(unroll):
            slot = group * unroll + k
            row = jnp.where(slot < count, plan[slot], spare)
            peer = plan[slots + slot]
            source = peer % PLANE * planes + peer // PLANE
            total[row] += jnp.dot(
                tiles_ref[slot], arrived_ref[source], preferred_element_type=jnp.float32
            )
        return carry

    lax.fori_loop(0, (count + unroll - 1) // unroll, steps, 0)
    line = lax.broadcasted_iota(jnp.int32, (EXTRA, TILE), 0)
    for holder in range(holders):
        exponents = jnp.zeros((EXTRA, TILE), jnp.float32)
        for b in range(blocks):
            value = total[holder * blocks + b]
            top = jnp.max(jnp.abs(value), axis=1, keepdims=True)
            exponent = jnp.ceil(jnp.log2(jnp.clip(top, 2.0**-100, 2.0**120)))
            scaled = value * (jnp.exp2(-exponent) * LEVELS)
            scaled = jnp.clip(jnp.round(scaled), -32767.0, 32767.0)
            coded_ref[holder, b * TILE : (b + 1) * TILE, :] = scaled.astype(jnp.int32).astype(jnp.int16)
            exponents = jnp.where(line == b, to_lanes(exponent), exponents)
        coded_ref[holder, blocks * TILE :, :] = exponents.astype(jnp.int32).astype(jnp.int16)


def decode(coded_ref, root_ref):
    holders, coded_rows, _ = coded_ref.shape
    blocks = (coded_rows - EXTRA) // TILE
    sums = [jnp.zeros((TILE, TILE), jnp.float32)] * blocks
    for holder in range(holders):
        exponents = coded_ref[holder, blocks * TILE :, :].astype(jnp.int32).astype(jnp.float32)
        for b in range(blocks):
            scale = jnp.exp2(to_sublanes(exponents[b : b + 1])) * (1.0 / LEVELS)
            value = coded_ref[holder, b * TILE : (b + 1) * TILE, :].astype(jnp.int32).astype(jnp.float32)
            sums[b] = sums[b] + value * scale
    return jnp.concatenate(sums, axis=0) * root_ref[...]


def middle_kernel(coded_ref, root_ref, image_ref, gram_ref, copies_ref):
    image = decode(coded_ref, root_ref)
    image_ref[...] = image
    write_copies((image * root_ref[...]).astype(jnp.bfloat16), copies_ref)
    gram_ref[...] = dot(image, image, 0, 0)


def last_kernel(coded_ref, root_ref, image_ref, gram_ref):
    image = decode(coded_ref, root_ref)
    image_ref[...] = image
    gram_ref[...] = dot(image, image, 0, 0)


def dot(a, b, a_dim, b_dim):
    return lax.dot_general(
        a,
        b,
        (((a_dim,), (b_dim,)), ((), ())),
        precision=lax.Precision.HIGHEST,
        preferred_element_type=jnp.float32,
    )


def inverse_cholesky(gram):
    size = gram.shape[0]
    band = (SUBLANES, size)
    lane = lax.broadcasted_iota(jnp.int32, band, 1)
    line = lax.broadcasted_iota(jnp.int32, band, 0)
    steps = range(size // SUBLANES)
    inner = range(SUBLANES)
    left = [gram[SUBLANES * k : SUBLANES * (k + 1)] for k in steps]
    result = []

    def spread(rows, column):
        return jnp.broadcast_to(rows[:, column : column + 1], band)

    for k in steps:
        start = SUBLANES * k
        cleared = (lane >= start) & (lane < start + SUBLANES)
        columns = [spread(left[k], start + t) for t in inner]
        entry = [[jnp.broadcast_to(columns[t][j : j + 1], band) if t >= j else None for t in inner] for j in inner]
        own = jnp.where(cleared, (lane == line + start).astype(jnp.float32), left[k])
        row = [jnp.broadcast_to(own[j : j + 1], band) for j in inner]
        factor = {}
        solved = [None] * SUBLANES
        final = [None] * SUBLANES
        for j in range(0, SUBLANES, 2):
            a, b, c = entry[j][j], entry[j][j + 1], entry[j + 1][j + 1]
            over = 1.0 / (a * c - b * b)
            rest = range(j + 2, SUBLANES)
            first = {t: c * entry[j][t] - b * entry[j + 1][t] for t in rest}
            second = {t: a * entry[j + 1][t] - b * entry[j][t] for t in rest}
            for t in rest:
                for u in range(t, SUBLANES):
                    entry[t][u] = entry[t][u] - (first[t] * entry[j][u] + second[t] * entry[j + 1][u]) * over
            for t in rest:
                factor[t, j], factor[t, j + 1] = first[t] * over, second[t] * over
                row[t] = row[t] - (factor[t, j] * row[j] + factor[t, j + 1] * row[j + 1])
            solved[j] = (c * row[j] - b * row[j + 1]) * over
            solved[j + 1] = (a * row[j + 1] - b * row[j]) * over
            ratio = b * (1.0 / a)
            final[j] = row[j] * lax.rsqrt(a)
            final[j + 1] = (row[j + 1] - ratio * row[j]) * lax.rsqrt(c - b * ratio)
        rows = final[0]
        for j in range(1, SUBLANES):
            rows = jnp.where(line == j, final[j], rows)
        result.append(jnp.where(lane < start + SUBLANES, rows, 0.0))
        for q in steps[k + 1 :]:
            column = [spread(left[q], start + j) for j in inner]
            for j in range(0, SUBLANES, 2):
                for t in range(j + 2, SUBLANES):
                    column[t] = column[t] - (factor[t, j] * column[j] + factor[t, j + 1] * column[j + 1])
            terms = [column[j] * solved[j] for j in inner]
            while len(terms) > 1:
                terms = [terms[i] + terms[i + 1] for i in range(0, len(terms), 2)]
            left[q] = jnp.where(cleared, 0.0, left[q]) - terms[0]
    return jnp.concatenate(result, axis=0)


def bases_kernel(scale, grams_ref, image_one_ref, image_two_ref, first_ref, second_ref):
    width = grams_ref.shape[0]
    inverse_one = inverse_cholesky(grams_ref[:, :width])
    partial_solve = dot(image_two_ref[...], inverse_one, 1, 1)
    first_ref[...] = dot(image_one_ref[...], inverse_one, 1, 1) * scale
    folded = dot(dot(inverse_one, grams_ref[:, width:], 1, 0), inverse_one, 1, 1)
    folded = 0.5 * (folded + folded.T)
    inverse_two = inverse_cholesky(folded)
    second_ref[...] = dot(partial_solve, inverse_two, 1, 1) * scale


def call(kernel, out_shape, n_scalars, n_inputs, scratch=()):
    single = isinstance(out_shape, jax.ShapeDtypeStruct)
    return pl.pallas_call(
        kernel,
        out_shape=out_shape,
        in_specs=[pl.BlockSpec(memory_space=pltpu.SMEM)] * n_scalars
        + [pl.BlockSpec(memory_space=pltpu.VMEM)] * n_inputs,
        out_specs=pl.BlockSpec(memory_space=pltpu.VMEM)
        if single
        else [pl.BlockSpec(memory_space=pltpu.VMEM)] * len(out_shape),
        scratch_shapes=list(scratch),
        compiler_params=pltpu.CompilerParams(vmem_limit_bytes=VMEM_LIMIT),
    )


def sum_over_devices(value, row_devices, col_devices):
    rows, width = value.shape
    share = rows // row_devices
    parts = lax.all_to_all(
        value.reshape(row_devices, share, width), "row", split_axis=0, concat_axis=0, tiled=True
    )
    part = jnp.sum(parts, axis=0)
    parts = lax.all_to_all(
        jnp.broadcast_to(part[None], (col_devices, share, width)), "col", split_axis=0, concat_axis=0, tiled=True
    )
    part = jnp.sum(parts, axis=0)
    parts = lax.all_to_all(
        jnp.broadcast_to(part[None], (row_devices, share, width)), "row", split_axis=0, concat_axis=0, tiled=True
    )
    return parts.reshape(rows, width)


def on_device(sketch, degrees, tiles, tile_rows, tile_peers, tile_counts, requests):
    rows_dev, width = sketch.shape
    row_devices = lax.axis_size("row")
    col_devices = lax.axis_size("col")
    blocks_dev = rows_dev // TILE
    group_blocks = col_devices * blocks_dev
    f32, bf16, i16 = jnp.float32, jnp.bfloat16, jnp.int16
    shape = jax.ShapeDtypeStruct
    own_tiles = tiles[0, 0]
    planes = row_devices // PLANE
    row = lax.axis_index("row").reshape(1)

    copies_shape = shape((planes, rows_dev, width), bf16)
    image_shape = shape((rows_dev, width), f32)
    copies, root = pl.pallas_call(
        first_panel_kernel,
        out_shape=(copies_shape, image_shape),
        in_specs=[pl.BlockSpec(memory_space=pltpu.VMEM), pl.BlockSpec(memory_space=pl.ANY)],
        out_specs=[pl.BlockSpec(memory_space=pltpu.VMEM)] * 2,
        scratch_shapes=[pltpu.VMEM((rows_dev, width), f32), pltpu.SemaphoreType.DMA],
        compiler_params=pltpu.CompilerParams(vmem_limit_bytes=VMEM_LIMIT),
    )(degrees.reshape(blocks_dev, TILE), sketch)

    mine = requests[0, 0]
    other = lax.ppermute(mine, "row", [(r, r ^ 1) for r in range(row_devices)])
    pair = jnp.concatenate([mine, other])
    tables = [pair]
    for shift in range(1, CHIPS_X):
        tables.append(
            lax.ppermute(
                pair,
                "row",
                [
                    (r, r // PLANE * PLANE + (r + shift * CORES) % PLANE)
                    for r in range(row_devices)
                ],
            )
        )
    wanted, plan = lax.optimization_barrier(
        (
            jnp.concatenate(tables),
            jnp.concatenate([tile_rows[0, 0], tile_peers[0, 0], tile_counts[0]]),
        )
    )
    lines = [[y * PLANE + g for y in range(planes)] for g in range(PLANE)]
    plane = [[y * PLANE + g for g in range(PLANE)] for y in range(planes)]

    outgoing_shape = shape((PLANE, planes, TILE, width), bf16)
    coded_shape = shape((col_devices, rows_dev + EXTRA, width), i16)
    gram_shape = shape((width, width), f32)
    total = pltpu.VMEM((group_blocks + 1, TILE, width), f32)

    def product(copies):
        panels = lax.all_to_all(
            copies, "row", split_axis=0, concat_axis=0, tiled=True, axis_index_groups=lines
        ).reshape(planes, blocks_dev, TILE, width)
        outgoing = call(select_kernel, outgoing_shape, 2, 1)(wanted, row, panels)
        arrived = lax.all_to_all(
            outgoing, "row", split_axis=0, concat_axis=0, tiled=True, axis_index_groups=plane
        ).reshape(row_devices, TILE, width)
        coded = call(product_kernel, coded_shape, 1, 2, [total])(plan, own_tiles, arrived)
        return lax.all_to_all(coded, "col", split_axis=0, concat_axis=0, tiled=True)

    terms = product(copies)
    image_one, gram_one, copies = call(
        middle_kernel, (image_shape, gram_shape, copies_shape), 0, 2
    )(terms, root)
    terms = product(copies)
    image_two, gram_two = call(last_kernel, (image_shape, gram_shape), 0, 2)(terms, root)

    grams = sum_over_devices(jnp.concatenate([gram_one, gram_two], axis=1), row_devices, col_devices)
    scale = (rows_dev * row_devices * col_devices) ** 0.5
    return call(functools.partial(bases_kernel, scale), (image_shape, image_shape), 0, 3)(
        grams, image_one, image_two
    )


def solution(mesh):
    return jax.shard_map(
        on_device,
        mesh=mesh,
        in_specs=(
            P(("row", "col"), None),
            P(("row", "col")),
            P("row", "col", None, None, None),
            P("row", "col", None),
            P("row", "col", None),
            P("row", "col"),
            P("row", "col", None),
        ),
        out_specs=(P(("row", "col"), None), P(("row", "col"), None)),
        check_vma=False,
    )
```

```python
import functools

import jax
import jax.numpy as jnp
from jax import lax
from jax.experimental import pallas as pl
from jax.experimental.pallas import tpu as pltpu
from jax.sharding import PartitionSpec as P

TILE = 128
EXTRA = 16
LEVELS = 32766.0
VMEM_LIMIT = 48 * 1024 * 1024
SUBLANES = 8
CORES = 2
CHIPS_X = 4
PLANE = CHIPS_X * CORES


def diagonal_mask():
    return lax.broadcasted_iota(jnp.int32, (TILE, TILE), 0) == lax.broadcasted_iota(
        jnp.int32, (TILE, TILE), 1
    )


def to_lanes(column):
    return jnp.sum(jnp.where(diagonal_mask(), column, 0.0), axis=0, keepdims=True)


def to_sublanes(lanes):
    return jnp.sum(jnp.where(diagonal_mask(), lanes, 0.0), axis=1, keepdims=True)


def write_copies(panel, copies_ref):
    for y in range(copies_ref.shape[0]):
        copies_ref[y] = panel


def first_panel_kernel(degrees_ref, sketch_ref, copies_ref, root_ref, sketch, arrival):
    copy = pltpu.make_async_copy(sketch_ref, sketch, arrival)
    copy.start()
    roots = lax.rsqrt(degrees_ref[...].astype(jnp.float32))
    for b in range(degrees_ref.shape[0]):
        column = to_sublanes(roots[b : b + 1])
        root_ref[b * TILE : (b + 1) * TILE] = jnp.broadcast_to(column, (TILE, root_ref.shape[1]))
    copy.wait()
    write_copies((sketch[...] * root_ref[...]).astype(jnp.bfloat16), copies_ref)


def select_kernel(wanted, row, panels_ref, outgoing_ref):
    planes = panels_ref.shape[0]
    place = row[0] % PLANE
    x = place // CORES
    rows = planes * PLANE
    for g in range(PLANE):
        shift = (x - g // CORES + CHIPS_X) % CHIPS_X
        side = (place + g) % CORES
        base = (shift * CORES + side) * rows + place
        for y in range(planes):
            outgoing_ref[g, y] = panels_ref[y, wanted[base + y * PLANE]]


def product_kernel(plan, tiles_ref, arrived_ref, coded_ref, total):
    unroll = 32
    slots = tiles_ref.shape[0]
    count = plan[2 * slots]
    holders, coded_rows, _ = coded_ref.shape
    blocks = (coded_rows - EXTRA) // TILE
    spare = holders * blocks
    planes = arrived_ref.shape[0] // PLANE
    total[...] = jnp.zeros_like(total)

    def steps(group, carry):
        for k in range(unroll):
            slot = group * unroll + k
            row = jnp.where(slot < count, plan[slot], spare)
            peer = plan[slots + slot]
            source = peer % PLANE * planes + peer // PLANE
            total[row] += jnp.dot(
                tiles_ref[slot], arrived_ref[source], preferred_element_type=jnp.float32
            )
        return carry

    lax.fori_loop(0, (count + unroll - 1) // unroll, steps, 0)
    line = lax.broadcasted_iota(jnp.int32, (EXTRA, TILE), 0)
    for holder in range(holders):
        exponents = jnp.zeros((EXTRA, TILE), jnp.float32)
        for b in range(blocks):
            value = total[holder * blocks + b]
            top = jnp.max(jnp.abs(value), axis=0, keepdims=True)
            column = jnp.ceil(jnp.log2(jnp.clip(top, 2.0**-100, 2.0**100)))
            value = value * jnp.exp2(-column)
            top = jnp.max(jnp.abs(value), axis=1, keepdims=True)
            row = jnp.ceil(jnp.log2(jnp.clip(top, 2.0**-60, 2.0)))
            scaled = value * (jnp.exp2(-row) * LEVELS)
            scaled = jnp.clip(jnp.round(scaled), -32767.0, 32767.0)
            coded_ref[holder, b * TILE : (b + 1) * TILE, :] = scaled.astype(jnp.int32).astype(jnp.int16)
            exponents = jnp.where(line == b, to_lanes(row), exponents)
            exponents = jnp.where(line == blocks + b, column, exponents)
        coded_ref[holder, blocks * TILE :, :] = exponents.astype(jnp.int32).astype(jnp.int16)


def decode(coded_ref, root_ref):
    holders, coded_rows, _ = coded_ref.shape
    blocks = (coded_rows - EXTRA) // TILE
    sums = [jnp.zeros((TILE, TILE), jnp.float32)] * blocks
    for holder in range(holders):
        exponents = coded_ref[holder, blocks * TILE :, :].astype(jnp.int32).astype(jnp.float32)
        for b in range(blocks):
            scale = jnp.exp2(to_sublanes(exponents[b : b + 1])) * (1.0 / LEVELS)
            scale = scale * jnp.exp2(exponents[blocks + b : blocks + b + 1])
            value = coded_ref[holder, b * TILE : (b + 1) * TILE, :].astype(jnp.int32).astype(jnp.float32)
            sums[b] = sums[b] + value * scale
    return jnp.concatenate(sums, axis=0) * root_ref[...]


def middle_kernel(coded_ref, root_ref, image_ref, gram_ref, copies_ref):
    image = decode(coded_ref, root_ref)
    image_ref[...] = image
    write_copies((image * root_ref[...]).astype(jnp.bfloat16), copies_ref)
    gram_ref[...] = dot(image, image, 0, 0)


def last_kernel(coded_ref, root_ref, image_ref, gram_ref):
    image = decode(coded_ref, root_ref)
    image_ref[...] = image
    gram_ref[...] = dot(image, image, 0, 0)


def dot(a, b, a_dim, b_dim):
    return lax.dot_general(
        a,
        b,
        (((a_dim,), (b_dim,)), ((), ())),
        precision=lax.Precision.HIGHEST,
        preferred_element_type=jnp.float32,
    )


def inverse_cholesky(gram):
    size = gram.shape[0]
    band = (SUBLANES, size)
    lane = lax.broadcasted_iota(jnp.int32, band, 1)
    line = lax.broadcasted_iota(jnp.int32, band, 0)
    steps = range(size // SUBLANES)
    inner = range(SUBLANES)
    left = [gram[SUBLANES * k : SUBLANES * (k + 1)] for k in steps]
    right = [(lane == line + SUBLANES * k).astype(jnp.float32) for k in steps]

    def spread(rows, column):
        return jnp.broadcast_to(rows[:, column : column + 1], band)

    for k in steps:
        start = SUBLANES * k
        row_left = [jnp.broadcast_to(left[k][j : j + 1], band) for j in inner]
        row_right = [jnp.broadcast_to(right[k][j : j + 1], band) for j in inner]
        entry = [[spread(row_left[j], start + t) if t >= j else None for t in inner] for j in inner]
        inverse = [None] * SUBLANES
        factor = [[None] * SUBLANES for _ in inner]
        for j in inner:
            inverse[j] = 1.0 / entry[j][j]
            for t in range(j + 1, SUBLANES):
                factor[t][j] = entry[j][t] * inverse[j]
                for u in range(t, SUBLANES):
                    entry[t][u] = entry[t][u] - factor[t][j] * entry[j][u]
                row_left[t] = row_left[t] - factor[t][j] * row_left[j]
                row_right[t] = row_right[t] - factor[t][j] * row_right[j]
        step_left = [row_left[j] * inverse[j] for j in inner]
        step_right = [row_right[j] * inverse[j] for j in inner]
        for q in steps[k + 1 :]:
            column = [spread(left[q], start + j) for j in inner]
            for j in inner:
                for t in range(j + 1, SUBLANES):
                    column[t] = column[t] - column[j] * factor[t][j]
            left[q] = left[q] - sum(column[j] * step_left[j] for j in inner)
            right[q] = right[q] - sum(column[j] * step_right[j] for j in inner)
        for j in inner:
            right[k] = jnp.where(line == j, row_right[j] * lax.rsqrt(entry[j][j]), right[k])
    return jnp.concatenate(right, axis=0)


def bases_kernel(scale, grams_ref, image_one_ref, image_two_ref, first_ref, second_ref):
    width = grams_ref.shape[0]
    inverse_one = inverse_cholesky(grams_ref[:, :width])
    partial_solve = dot(image_two_ref[...], inverse_one, 1, 1)
    first_ref[...] = dot(image_one_ref[...], inverse_one, 1, 1) * scale
    folded = dot(dot(inverse_one, grams_ref[:, width:], 1, 0), inverse_one, 1, 1)
    folded = 0.5 * (folded + folded.T)
    inverse_two = inverse_cholesky(folded)
    second_ref[...] = dot(partial_solve, inverse_two, 1, 1) * scale


def call(kernel, out_shape, n_scalars, n_inputs, scratch=()):
    single = isinstance(out_shape, jax.ShapeDtypeStruct)
    return pl.pallas_call(
        kernel,
        out_shape=out_shape,
        in_specs=[pl.BlockSpec(memory_space=pltpu.SMEM)] * n_scalars
        + [pl.BlockSpec(memory_space=pltpu.VMEM)] * n_inputs,
        out_specs=pl.BlockSpec(memory_space=pltpu.VMEM)
        if single
        else [pl.BlockSpec(memory_space=pltpu.VMEM)] * len(out_shape),
        scratch_shapes=list(scratch),
        compiler_params=pltpu.CompilerParams(vmem_limit_bytes=VMEM_LIMIT),
    )


def sum_over_devices(value, row_devices, col_devices):
    rows, width = value.shape
    share = rows // row_devices
    parts = lax.all_to_all(
        value.reshape(row_devices, share, width), "row", split_axis=0, concat_axis=0, tiled=True
    )
    part = jnp.sum(parts, axis=0)
    parts = lax.all_to_all(
        jnp.broadcast_to(part[None], (col_devices, share, width)), "col", split_axis=0, concat_axis=0, tiled=True
    )
    part = jnp.sum(parts, axis=0)
    parts = lax.all_to_all(
        jnp.broadcast_to(part[None], (row_devices, share, width)), "row", split_axis=0, concat_axis=0, tiled=True
    )
    return parts.reshape(rows, width)


def on_device(sketch, degrees, tiles, tile_rows, tile_peers, tile_counts, requests):
    rows_dev, width = sketch.shape
    row_devices = lax.axis_size("row")
    col_devices = lax.axis_size("col")
    blocks_dev = rows_dev // TILE
    group_blocks = col_devices * blocks_dev
    f32, bf16, i16 = jnp.float32, jnp.bfloat16, jnp.int16
    shape = jax.ShapeDtypeStruct
    own_tiles = tiles[0, 0]
    planes = row_devices // PLANE
    row = lax.axis_index("row").reshape(1)

    copies_shape = shape((planes, rows_dev, width), bf16)
    image_shape = shape((rows_dev, width), f32)
    copies, root = pl.pallas_call(
        first_panel_kernel,
        out_shape=(copies_shape, image_shape),
        in_specs=[pl.BlockSpec(memory_space=pltpu.VMEM), pl.BlockSpec(memory_space=pl.ANY)],
        out_specs=[pl.BlockSpec(memory_space=pltpu.VMEM)] * 2,
        scratch_shapes=[pltpu.VMEM((rows_dev, width), f32), pltpu.SemaphoreType.DMA],
        compiler_params=pltpu.CompilerParams(vmem_limit_bytes=VMEM_LIMIT),
    )(degrees.reshape(blocks_dev, TILE), sketch)

    mine = requests[0, 0]
    other = lax.ppermute(mine, "row", [(r, r ^ 1) for r in range(row_devices)])
    pair = jnp.concatenate([mine, other])
    tables = [pair]
    for shift in range(1, CHIPS_X):
        tables.append(
            lax.ppermute(
                pair,
                "row",
                [
                    (r, r // PLANE * PLANE + (r + shift * CORES) % PLANE)
                    for r in range(row_devices)
                ],
            )
        )
    wanted, plan = lax.optimization_barrier(
        (
            jnp.concatenate(tables),
            jnp.concatenate([tile_rows[0, 0], tile_peers[0, 0], tile_counts[0]]),
        )
    )
    lines = [[y * PLANE + g for y in range(planes)] for g in range(PLANE)]
    plane = [[y * PLANE + g for g in range(PLANE)] for y in range(planes)]

    outgoing_shape = shape((PLANE, planes, TILE, width), bf16)
    coded_shape = shape((col_devices, rows_dev + EXTRA, width), i16)
    gram_shape = shape((width, width), f32)
    total = pltpu.VMEM((group_blocks + 1, TILE, width), f32)

    def product(copies):
        panels = lax.all_to_all(
            copies, "row", split_axis=0, concat_axis=0, tiled=True, axis_index_groups=lines
        ).reshape(planes, blocks_dev, TILE, width)
        outgoing = call(select_kernel, outgoing_shape, 2, 1)(wanted, row, panels)
        arrived = lax.all_to_all(
            outgoing, "row", split_axis=0, concat_axis=0, tiled=True, axis_index_groups=plane
        ).reshape(row_devices, TILE, width)
        coded = call(product_kernel, coded_shape, 1, 2, [total])(plan, own_tiles, arrived)
        return lax.all_to_all(coded, "col", split_axis=0, concat_axis=0, tiled=True)

    terms = product(copies)
    image_one, gram_one, copies = call(
        middle_kernel, (image_shape, gram_shape, copies_shape), 0, 2
    )(terms, root)
    terms = product(copies)
    image_two, gram_two = call(last_kernel, (image_shape, gram_shape), 0, 2)(terms, root)

    grams = sum_over_devices(jnp.concatenate([gram_one, gram_two], axis=1), row_devices, col_devices)
    scale = (rows_dev * row_devices * col_devices) ** 0.5
    return call(functools.partial(bases_kernel, scale), (image_shape, image_shape), 0, 3)(
        grams, image_one, image_two
    )


def solution(mesh):
    return jax.shard_map(
        on_device,
        mesh=mesh,
        in_specs=(
            P(("row", "col"), None),
            P(("row", "col")),
            P("row", "col", None, None, None),
            P("row", "col", None),
            P("row", "col", None),
            P("row", "col"),
            P("row", "col", None),
        ),
        out_specs=(P(("row", "col"), None), P(("row", "col"), None)),
        check_vma=False,
    )
```

```python
import functools

import jax
import jax.numpy as jnp
from jax import lax
from jax.experimental import pallas as pl
from jax.experimental.pallas import tpu as pltpu
from jax.sharding import PartitionSpec as P

TILE = 128
EXTRA = 16
LEVELS = 32766.0
VMEM_LIMIT = 48 * 1024 * 1024
SUBLANES = 8
CORES = 2
CHIPS_X = 4
PLANE = CHIPS_X * CORES


def diagonal_mask():
    return lax.broadcasted_iota(jnp.int32, (TILE, TILE), 0) == lax.broadcasted_iota(
        jnp.int32, (TILE, TILE), 1
    )


def to_lanes(column):
    return jnp.sum(jnp.where(diagonal_mask(), column, 0.0), axis=0, keepdims=True)


def to_sublanes(lanes):
    return jnp.sum(jnp.where(diagonal_mask(), lanes, 0.0), axis=1, keepdims=True)


def write_copies(panel, copies_ref):
    for y in range(copies_ref.shape[0]):
        copies_ref[y] = panel


def first_panel_kernel(degrees_ref, sketch_ref, copies_ref, root_ref, sketch, arrival):
    copy = pltpu.make_async_copy(sketch_ref, sketch, arrival)
    copy.start()
    roots = lax.rsqrt(degrees_ref[...].astype(jnp.float32))
    for b in range(degrees_ref.shape[0]):
        column = to_sublanes(roots[b : b + 1])
        root_ref[b * TILE : (b + 1) * TILE] = jnp.broadcast_to(column, (TILE, root_ref.shape[1]))
    copy.wait()
    write_copies((sketch[...] * root_ref[...]).astype(jnp.bfloat16), copies_ref)


def select_kernel(wanted, row, panels_ref, outgoing_ref):
    planes = panels_ref.shape[0]
    place = row[0] % PLANE
    x = place // CORES
    rows = planes * PLANE
    for g in range(PLANE):
        shift = (x - g // CORES + CHIPS_X) % CHIPS_X
        side = (place + g) % CORES
        base = (shift * CORES + side) * rows + place
        for y in range(planes):
            outgoing_ref[g, y] = panels_ref[y, wanted[base + y * PLANE]]


def product_kernel(plan, tiles_ref, arrived_ref, coded_ref, total):
    unroll = 32
    slots = tiles_ref.shape[0]
    count = plan[2 * slots]
    holders, coded_rows, _ = coded_ref.shape
    blocks = (coded_rows - EXTRA) // TILE
    spare = holders * blocks
    planes = arrived_ref.shape[0] // PLANE
    total[...] = jnp.zeros_like(total)

    def steps(group, carry):
        for k in range(unroll):
            slot = group * unroll + k
            row = jnp.where(slot < count, plan[slot], spare)
            peer = plan[slots + slot]
            source = peer % PLANE * planes + peer // PLANE
            total[row] += jnp.dot(
                tiles_ref[slot], arrived_ref[source], preferred_element_type=jnp.float32
            )
        return carry

    lax.fori_loop(0, (count + unroll - 1) // unroll, steps, 0)
    line = lax.broadcasted_iota(jnp.int32, (EXTRA, TILE), 0)
    for holder in range(holders):
        exponents = jnp.zeros((EXTRA, TILE), jnp.float32)
        for b in range(blocks):
            value = total[holder * blocks + b]
            top = jnp.max(jnp.abs(value), axis=0, keepdims=True)
            column = jnp.ceil(jnp.log2(jnp.clip(top, 2.0**-100, 2.0**100)))
            value = value * jnp.exp2(-column)
            top = jnp.max(jnp.abs(value), axis=1, keepdims=True)
            row = jnp.ceil(jnp.log2(jnp.clip(top, 2.0**-60, 2.0)))
            scaled = value * (jnp.exp2(-row) * LEVELS)
            scaled = jnp.clip(jnp.round(scaled), -32767.0, 32767.0)
            coded_ref[holder, b * TILE : (b + 1) * TILE, :] = scaled.astype(jnp.int32).astype(jnp.int16)
            exponents = jnp.where(line == b, to_lanes(row), exponents)
            exponents = jnp.where(line == blocks + b, column, exponents)
        coded_ref[holder, blocks * TILE :, :] = exponents.astype(jnp.int32).astype(jnp.int16)


def decode(coded_ref, root_ref):
    holders, coded_rows, _ = coded_ref.shape
    blocks = (coded_rows - EXTRA) // TILE
    sums = [jnp.zeros((TILE, TILE), jnp.float32)] * blocks
    for holder in range(holders):
        exponents = coded_ref[holder, blocks * TILE :, :].astype(jnp.int32).astype(jnp.float32)
        for b in range(blocks):
            scale = jnp.exp2(to_sublanes(exponents[b : b + 1])) * (1.0 / LEVELS)
            scale = scale * jnp.exp2(exponents[blocks + b : blocks + b + 1])
            value = coded_ref[holder, b * TILE : (b + 1) * TILE, :].astype(jnp.int32).astype(jnp.float32)
            sums[b] = sums[b] + value * scale
    return jnp.concatenate(sums, axis=0) * root_ref[...]


def middle_kernel(coded_ref, root_ref, image_ref, gram_ref, copies_ref):
    image = decode(coded_ref, root_ref)
    image_ref[...] = image
    write_copies((image * root_ref[...]).astype(jnp.bfloat16), copies_ref)
    gram_ref[...] = dot(image, image, 0, 0)


def last_kernel(coded_ref, root_ref, image_ref, gram_ref):
    image = decode(coded_ref, root_ref)
    image_ref[...] = image
    gram_ref[...] = dot(image, image, 0, 0)


def dot(a, b, a_dim, b_dim):
    return lax.dot_general(
        a,
        b,
        (((a_dim,), (b_dim,)), ((), ())),
        precision=lax.Precision.HIGHEST,
        preferred_element_type=jnp.float32,
    )


def inverse_cholesky(gram):
    size = gram.shape[0]
    unit = lax.rsqrt(jnp.sum(jnp.where(diagonal_mask(), gram, 0.0), axis=0, keepdims=True))
    gram = gram * unit * to_sublanes(unit)
    band = (SUBLANES, size)
    lane = lax.broadcasted_iota(jnp.int32, band, 1)
    line = lax.broadcasted_iota(jnp.int32, band, 0)
    steps = range(size // SUBLANES)
    inner = range(SUBLANES)
    left = [gram[SUBLANES * k : SUBLANES * (k + 1)] for k in steps]
    result = []

    def spread(rows, column):
        return jnp.broadcast_to(rows[:, column : column + 1], band)

    for k in steps:
        start = SUBLANES * k
        cleared = (lane >= start) & (lane < start + SUBLANES)
        columns = [spread(left[k], start + t) for t in inner]
        entry = [[jnp.broadcast_to(columns[t][j : j + 1], band) if t >= j else None for t in inner] for j in inner]
        own = jnp.where(cleared, (lane == line + start).astype(jnp.float32), left[k])
        row = [jnp.broadcast_to(own[j : j + 1], band) for j in inner]
        factor = {}
        solved = [None] * SUBLANES
        final = [None] * SUBLANES
        for j in range(0, SUBLANES, 2):
            a, b, c = entry[j][j], entry[j][j + 1], entry[j + 1][j + 1]
            over = 1.0 / (a * c - b * b)
            rest = range(j + 2, SUBLANES)
            first = {t: c * entry[j][t] - b * entry[j + 1][t] for t in rest}
            second = {t: a * entry[j + 1][t] - b * entry[j][t] for t in rest}
            for t in rest:
                for u in range(t, SUBLANES):
                    entry[t][u] = entry[t][u] - (first[t] * entry[j][u] + second[t] * entry[j + 1][u]) * over
            for t in rest:
                factor[t, j], factor[t, j + 1] = first[t] * over, second[t] * over
                row[t] = row[t] - (factor[t, j] * row[j] + factor[t, j + 1] * row[j + 1])
            solved[j] = (c * row[j] - b * row[j + 1]) * over
            solved[j + 1] = (a * row[j + 1] - b * row[j]) * over
            ratio = b * (1.0 / a)
            final[j] = row[j] * lax.rsqrt(a)
            final[j + 1] = (row[j + 1] - ratio * row[j]) * lax.rsqrt(c - b * ratio)
        rows = final[0]
        for j in range(1, SUBLANES):
            rows = jnp.where(line == j, final[j], rows)
        result.append(jnp.where(lane < start + SUBLANES, rows, 0.0))
        for q in steps[k + 1 :]:
            column = [spread(left[q], start + j) for j in inner]
            for j in range(0, SUBLANES, 2):
                for t in range(j + 2, SUBLANES):
                    column[t] = column[t] - (factor[t, j] * column[j] + factor[t, j + 1] * column[j + 1])
            terms = [column[j] * solved[j] for j in inner]
            while len(terms) > 1:
                terms = [terms[i] + terms[i + 1] for i in range(0, len(terms), 2)]
            left[q] = jnp.where(cleared, 0.0, left[q]) - terms[0]
    return jnp.concatenate(result, axis=0) * unit


def bases_kernel(scale, grams_ref, image_one_ref, image_two_ref, first_ref, second_ref):
    width = grams_ref.shape[0]
    inverse_one = inverse_cholesky(grams_ref[:, :width])
    partial_solve = dot(image_two_ref[...], inverse_one, 1, 1)
    first_ref[...] = dot(image_one_ref[...], inverse_one, 1, 1) * scale
    folded = dot(dot(inverse_one, grams_ref[:, width:], 1, 0), inverse_one, 1, 1)
    folded = 0.5 * (folded + folded.T)
    inverse_two = inverse_cholesky(folded)
    second_ref[...] = dot(partial_solve, inverse_two, 1, 1) * scale


def call(kernel, out_shape, n_scalars, n_inputs, scratch=()):
    single = isinstance(out_shape, jax.ShapeDtypeStruct)
    return pl.pallas_call(
        kernel,
        out_shape=out_shape,
        in_specs=[pl.BlockSpec(memory_space=pltpu.SMEM)] * n_scalars
        + [pl.BlockSpec(memory_space=pltpu.VMEM)] * n_inputs,
        out_specs=pl.BlockSpec(memory_space=pltpu.VMEM)
        if single
        else [pl.BlockSpec(memory_space=pltpu.VMEM)] * len(out_shape),
        scratch_shapes=list(scratch),
        compiler_params=pltpu.CompilerParams(vmem_limit_bytes=VMEM_LIMIT),
    )


def sum_over_devices(value, row_devices, col_devices):
    rows, width = value.shape
    share = rows // row_devices
    parts = lax.all_to_all(
        value.reshape(row_devices, share, width), "row", split_axis=0, concat_axis=0, tiled=True
    )
    part = jnp.sum(parts, axis=0)
    parts = lax.all_to_all(
        jnp.broadcast_to(part[None], (col_devices, share, width)), "col", split_axis=0, concat_axis=0, tiled=True
    )
    part = jnp.sum(parts, axis=0)
    parts = lax.all_to_all(
        jnp.broadcast_to(part[None], (row_devices, share, width)), "row", split_axis=0, concat_axis=0, tiled=True
    )
    return parts.reshape(rows, width)


def on_device(sketch, degrees, tiles, tile_rows, tile_peers, tile_counts, requests):
    rows_dev, width = sketch.shape
    row_devices = lax.axis_size("row")
    col_devices = lax.axis_size("col")
    blocks_dev = rows_dev // TILE
    group_blocks = col_devices * blocks_dev
    f32, bf16, i16 = jnp.float32, jnp.bfloat16, jnp.int16
    shape = jax.ShapeDtypeStruct
    own_tiles = tiles[0, 0]
    planes = row_devices // PLANE
    row = lax.axis_index("row").reshape(1)

    copies_shape = shape((planes, rows_dev, width), bf16)
    image_shape = shape((rows_dev, width), f32)
    copies, root = pl.pallas_call(
        first_panel_kernel,
        out_shape=(copies_shape, image_shape),
        in_specs=[pl.BlockSpec(memory_space=pltpu.VMEM), pl.BlockSpec(memory_space=pl.ANY)],
        out_specs=[pl.BlockSpec(memory_space=pltpu.VMEM)] * 2,
        scratch_shapes=[pltpu.VMEM((rows_dev, width), f32), pltpu.SemaphoreType.DMA],
        compiler_params=pltpu.CompilerParams(vmem_limit_bytes=VMEM_LIMIT),
    )(degrees.reshape(blocks_dev, TILE), sketch)

    mine = requests[0, 0]
    other = lax.ppermute(mine, "row", [(r, r ^ 1) for r in range(row_devices)])
    pair = jnp.concatenate([mine, other])
    tables = [pair]
    for shift in range(1, CHIPS_X):
        tables.append(
            lax.ppermute(
                pair,
                "row",
                [
                    (r, r // PLANE * PLANE + (r + shift * CORES) % PLANE)
                    for r in range(row_devices)
                ],
            )
        )
    wanted, plan = lax.optimization_barrier(
        (
            jnp.concatenate(tables),
            jnp.concatenate([tile_rows[0, 0], tile_peers[0, 0], tile_counts[0]]),
        )
    )
    lines = [[y * PLANE + g for y in range(planes)] for g in range(PLANE)]
    plane = [[y * PLANE + g for g in range(PLANE)] for y in range(planes)]

    outgoing_shape = shape((PLANE, planes, TILE, width), bf16)
    coded_shape = shape((col_devices, rows_dev + EXTRA, width), i16)
    gram_shape = shape((width, width), f32)
    total = pltpu.VMEM((group_blocks + 1, TILE, width), f32)

    def product(copies):
        panels = lax.all_to_all(
            copies, "row", split_axis=0, concat_axis=0, tiled=True, axis_index_groups=lines
        ).reshape(planes, blocks_dev, TILE, width)
        outgoing = call(select_kernel, outgoing_shape, 2, 1)(wanted, row, panels)
        arrived = lax.all_to_all(
            outgoing, "row", split_axis=0, concat_axis=0, tiled=True, axis_index_groups=plane
        ).reshape(row_devices, TILE, width)
        coded = call(product_kernel, coded_shape, 1, 2, [total])(plan, own_tiles, arrived)
        return lax.all_to_all(coded, "col", split_axis=0, concat_axis=0, tiled=True)

    terms = product(copies)
    image_one, gram_one, copies = call(
        middle_kernel, (image_shape, gram_shape, copies_shape), 0, 2
    )(terms, root)
    terms = product(copies)
    image_two, gram_two = call(last_kernel, (image_shape, gram_shape), 0, 2)(terms, root)

    grams = sum_over_devices(jnp.concatenate([gram_one, gram_two], axis=1), row_devices, col_devices)
    scale = (rows_dev * row_devices * col_devices) ** 0.5
    return call(functools.partial(bases_kernel, scale), (image_shape, image_shape), 0, 3)(
        grams, image_one, image_two
    )


def solution(mesh):
    return jax.shard_map(
        on_device,
        mesh=mesh,
        in_specs=(
            P(("row", "col"), None),
            P(("row", "col")),
            P("row", "col", None, None, None),
            P("row", "col", None),
            P("row", "col", None),
            P("row", "col"),
            P("row", "col", None),
        ),
        out_specs=(P(("row", "col"), None), P(("row", "col"), None)),
        check_vma=False,
    )
```
